32 devices in a mesh: dp: 4 (over x, core), segment: 2 (over y), seq: 4 (over z).
Axes of the slice: x: 2, y: 2, z: 4, core: 2. Of those that a mesh axis runs over, the one named last changes fastest.
Arguments:
- activations: bfloat16 [4, 4, 512, 768], P('dp', None, 'seq'), may hold values from -6 to 6
- conv_weight: bfloat16 [2, 5, 768, 768], P('segment', None, ('dp', 'seq')), may hold values from -0.125 to 0.125
- norm_gain: float32 [2, 768], P('segment'), may hold values from 0.25 to 1.75
- conv_bias: float32 [2, 768], P('segment'), may hold values from -3 to 3
Outputs:
- block_outputs: bfloat16 [2, 4, 4, 512, 768], P('segment', 'dp', None, 'seq')
The draws below stay inside these ranges and needn't reach their ends.
All inputs are finite; a program needn't handle non-finite values.
Results may differ from the reference program's by a relative error of at most 0.0065.
Values may be sent and summed in bfloat16 or wider, within the bound.
A program may use at most 64 MiB of HBM per device.

```python
import jax
import jax.numpy as jnp
from jax import lax

C = 768
KW = 5
M = 4
L = 512
BATCH = 4
SEGMENTS = 2


def block_scale(stream_key, dims, shards, smallest, high):
    loudness, own = 1.0, jax.random.fold_in(stream_key, 6)
    for axis_at, blocks in shards:
        steps = jnp.exp(jax.random.uniform(jax.random.fold_in(own, axis_at), (blocks,), jnp.float32, smallest / len(shards), high / len(shards)))
        loudness = loudness * jnp.repeat(steps, dims[axis_at] // blocks).reshape([-1 if axis == axis_at else 1 for axis in range(len(dims))])
    return loudness


def gaussian(stream_key, extent, width, limit, split=(), held_as=jnp.bfloat16):
    array = width * jax.random.normal(stream_key, extent, jnp.float32)
    if split:
        array = array * block_scale(stream_key, extent, split, -0.22, 0.18)
    return jnp.clip(array, -limit, limit).astype(held_as)


def setup_inputs(seed: int = 0) -> dict:
    key_of = jax.random.split(jax.random.key(seed), 5)
    activations = gaussian(key_of[0], (BATCH, M, L, C), 1.0, 6.0, ((0, 4), (2, 4)))
    conv_weight = gaussian(key_of[1], (SEGMENTS, KW, C, C), (KW * C // 2) ** -0.5, 0.125, ((0, 2), (2, 16)))
    norm_gain = jnp.clip(1.0 + 0.15 * jax.random.normal(key_of[2], (SEGMENTS, C), jnp.float32), 0.25, 1.75)
    conv_bias = gaussian(key_of[3], (SEGMENTS, C), 0.5, 3.0, ((0, 2),), jnp.float32)
    return {"activations": activations, "conv_weight": conv_weight, "norm_gain": norm_gain, "conv_bias": conv_bias}


def block(rows, weight, gain, bias):
    wide = rows.astype(jnp.float32)
    stat = lax.optimization_barrier(jnp.mean(wide * wide, axis=-1, keepdims=True))
    normed = (wide / jnp.sqrt(stat + 1e-06) * gain).astype(jnp.bfloat16)
    padded = jnp.pad(normed, ((2, 2), (0, 0)))
    length = rows.shape[0]
    total = jnp.zeros((length, weight.shape[2]), jnp.float32)
    for tap in range(KW):
        total = total + jnp.dot(padded[tap:tap + length], weight[tap], preferred_element_type=jnp.float32)
    return wide + jax.nn.gelu(total + bias, approximate=True)

def reference(activations, conv_weight, norm_gain, conv_bias):
    results = []
    for segment in range(SEGMENTS):
        results.append([])
    for slot in range(BATCH):
        for micro in range(M):
            current = activations[slot, micro]
            first = None
            for segment in range(SEGMENTS):
                lifted = block(current, conv_weight[segment], norm_gain[segment], conv_bias[segment])
                if segment == SEGMENTS - 1:
                    final = (lifted + first.astype(jnp.float32)).astype(jnp.bfloat16)
                    results[segment].append(final)
                else:
                    current = lifted.astype(jnp.bfloat16)
                    if segment == 0:
                        first = current
                    results[segment].append(current)
    stacked = [jnp.stack(items).reshape(BATCH, M, L, C) for items in results]
    return jnp.stack(stacked)
```

```python
import functools

import jax
import jax.numpy as jnp
from jax import lax
from jax.experimental import pallas as pl
from jax.experimental.pallas import tpu as pltpu
from jax.sharding import PartitionSpec as P

EDGE = 16
HALF = 128
WIDE = 256
SIB, ACROSS, UP, DOWN = range(4)


def column_chunks(width):
    blocks = width // WIDE
    chunks = [(0, 0, 0, HALF, True)]
    for block in range(1, blocks):
        chunks.append((block, 0, HALF + (block - 1) * WIDE, WIDE, False))
    chunks.append((0, HALF, width - HALF, HALF, False))
    return chunks


def kernel(
    seqs, act, weight, gain, bias, out,
    xin, halo, wbuf, padded, shifted,
    load_sem, own_sem, wsend, wrecv, hsend, hrecv, rsend, rrecv, esend, erecv,
):
    micros, rows, width = xin.shape
    taps = weight.shape[1]
    depth = weight.shape[2]
    chunks = column_chunks(width)
    dp = lax.axis_index("dp")
    seg = lax.axis_index("segment")
    z = lax.axis_index("seq")
    chip, core = dp // 2, dp % 2
    sib = chip * 2 + (1 - core)
    across = (1 - chip) * 2 + core
    has_up = z + 1 < seqs
    has_down = z > 0
    first = seg == 0

    def always(body):
        body()

    def when(*conds):
        conds = [c for c in conds if c is not None]
        if not conds:
            return always
        return pl.when(functools.reduce(jnp.logical_and, conds))

    targets = {
        SIB: (None, (sib, seg, z)),
        ACROSS: (None, (across, seg, z)),
        UP: (has_up, (dp, seg, z + 1)),
        DOWN: (has_down, (dp, seg, z - 1)),
    }

    barrier = pltpu.get_barrier_semaphore()

    def greet(device):
        pl.semaphore_signal(barrier, inc=1, device_id=device, device_id_type=pl.DeviceIdType.MESH)

    greet((sib, seg, z))
    greet((across, seg, z))
    greet((dp, 1 - seg, z))

    @pl.when(has_up)
    def _():
        greet((dp, seg, z + 1))
        greet((dp, 1 - seg, z + 1))

    @pl.when(has_down)
    def _():
        greet((dp, seg, z - 1))
        greet((dp, 1 - seg, z - 1))

    own_w = []
    for j, (b, bc, c0, cw, _) in enumerate(chunks):
        start = pl.multiple_of((dp * seqs + z) * depth, EDGE)
        own_w.append(
            pltpu.make_async_copy(
                weight.at[0, :, :, pl.ds(c0, cw)],
                wbuf.at[b, :, pl.ds(start, depth), pl.ds(bc, cw)],
                own_sem.at[j],
            )
        )
        own_w[-1].start()
    load_x = pltpu.make_async_copy(act.at[0], xin, load_sem)

    @pl.when(first)
    def _():
        load_x.start()

    ends = jnp.int32(has_up) + jnp.int32(has_down)
    pl.semaphore_wait(barrier, 3 + 2 * ends)

    pending = []

    def piece(j, owner, at):
        b, bc, _, cw, _ = chunks[j]
        start = pl.multiple_of((owner * seqs + at) * depth, EDGE)
        return wbuf.at[b, :, pl.ds(start, depth), pl.ds(bc, cw)]

    def transfer(j, owner, at, slot, way, own):
        c0, cw = chunks[j][2:4]
        dst = piece(j, owner, at)
        return pltpu.make_async_remote_copy(
            src_ref=weight.at[0, :, :, pl.ds(c0, cw)] if own else dst,
            dst_ref=dst,
            send_sem=wsend.at[j, slot * 4 + way],
            recv_sem=wrecv.at[j, owner * seqs + at],
            device_id=targets[way][1],
            device_id_type=pl.DeviceIdType.MESH,
        )

    def spread(j, owner, at, slot, ways, own=False, cond=None):
        for way in ways:
            make = functools.partial(transfer, j, owner, at, slot, way, own)

            @when(targets[way][0])
            def _():
                make().start()

            pending.append((cond, targets[way][0], make))

    def arrive(j, owner, at):
        transfer(j, owner, at, 0, SIB, False).wait_recv()

    def send_own(j):
        spread(j, dp, z, z, (ACROSS, UP, DOWN, SIB), own=True)

    def relay_weights(j):
        x_first = chunks[j][4]
        if x_first:
            arrive(j, across, z)
            spread(j, across, z, seqs + z, (UP, DOWN, SIB))
        else:
            arrive(j, across, z)
            spread(j, across, z, seqs + z, (SIB,))
        for d in range(1, seqs):
            for there, way in ((z - d, UP), (z + d, DOWN)):
                cond = there >= 0 if way == UP else there < seqs
                other = seqs + there

                @pl.when(cond)
                def _():
                    if x_first:
                        arrive(j, dp, there)
                        spread(j, dp, there, there, (way, SIB), cond=cond)
                        arrive(j, across, there)
                        spread(j, across, there, other, (way, SIB), cond=cond)
                    else:
                        arrive(j, dp, there)
                        spread(j, dp, there, there, (way, ACROSS, SIB), cond=cond)

            if not x_first:
                for there, cond in ((z - d, z - d >= 0), (z + d, z + d < seqs)):
                    other = seqs + there

                    @pl.when(cond)
                    def _():
                        arrive(j, across, there)
                        spread(j, across, there, other, (SIB,), cond=cond)

    def from_sibling(j):
        for at in range(seqs):
            arrive(j, sib, at)
            arrive(j, (1 - chip) * 2 + (1 - core), at)

    def edge_in(side):
        up = side == 0
        return pltpu.make_async_remote_copy(
            src_ref=act.at[0, :, pl.ds(rows - EDGE if up else 0, EDGE), :],
            dst_ref=halo.at[side],
            send_sem=hsend.at[side],
            recv_sem=hrecv.at[side],
            device_id=(dp, seg, z + 1 if up else z - 1),
            device_id_type=pl.DeviceIdType.MESH,
        )

    def edge_out(j, side):
        up = side == 0
        cols = pl.ds(chunks[j][2], chunks[j][3])
        return pltpu.make_async_remote_copy(
            src_ref=out.at[0, 0, :, pl.ds(rows - EDGE if up else 0, EDGE), cols],
            dst_ref=halo.at[side, :, :, cols],
            send_sem=esend.at[j, side],
            recv_sem=erecv.at[j, side],
            device_id=(dp, 1 - seg, z + 1 if up else z - 1),
            device_id_type=pl.DeviceIdType.MESH,
        )

    def rows_out(j):
        cols = pl.ds(chunks[j][2], chunks[j][3])
        return pltpu.make_async_remote_copy(
            src_ref=out.at[0, 0, :, :, cols],
            dst_ref=xin.at[:, :, cols],
            send_sem=rsend.at[j],
            recv_sem=rrecv.at[j],
            device_id=(dp, 1 - seg, z),
            device_id_type=pl.DeviceIdType.MESH,
        )

    for side, cond in ((0, z == 0), (1, z == seqs - 1)):

        @pl.when(cond)
        def _():
            halo[side] = jnp.zeros(halo.shape[1:], halo.dtype)

    def normed(cells):
        wide = cells.astype(jnp.float32)
        stat = jnp.mean(wide * wide, axis=-1, keepdims=True)
        return wide * lax.rsqrt(stat + 1e-06) * gain[...]

    def shift_rows():
        def one(m, carry):
            padded[m, pl.ds(0, EDGE)] = normed(halo[0, m])
            padded[m, pl.ds(EDGE, rows)] = normed(xin[m])
            padded[m, pl.ds(EDGE + rows, EDGE)] = normed(halo[1, m])
            at = pl.multiple_of(m * rows, rows)
            for tap in range(taps):
                shifted[pl.ds(at, rows), pl.ds(tap * width, width)] = padded[
                    m, pl.ds(EDGE - taps // 2 + tap, rows), :
                ].astype(jnp.bfloat16)
            return carry

        lax.fori_loop(0, micros, one, 0)

    def convolve(b, bc, cw):
        kern = wbuf[b, :, :, pl.ds(bc, cw)].reshape(taps * width, cw)
        return jnp.dot(shifted[...], kern, preferred_element_type=jnp.float32)

    def finish(total, c0, cw, join):
        cols = pl.ds(c0, cw)
        wide = xin[:, :, cols].astype(jnp.float32)
        total = total.reshape(micros, rows, cw) + bias[:, cols].reshape(1, 1, cw)
        lifted = wide + jax.nn.gelu(total, approximate=True)
        if join:
            lifted = lifted + wide
        out[0, 0, :, :, cols] = lifted.astype(out.dtype)

    send_own(0)

    @pl.when(first)
    def _():
        for side, cond in ((0, has_up), (1, has_down)):

            @pl.when(cond)
            def _():
                edge_in(side).start()

    send_own(1)

    @pl.when(first)
    def _():
        load_x.wait()
        for side, cond in ((0, has_down), (1, has_up)):

            @pl.when(cond)
            def _():
                edge_in(side).wait_recv()

        shift_rows()

    for copy in own_w:
        copy.wait()
    for j, (b, bc, c0, cw, _) in enumerate(chunks):
        relay_weights(j)
        if j + 2 < len(chunks):
            send_own(j + 2)
        from_sibling(j)

        @pl.when(first)
        def _():
            finish(convolve(b, bc, cw), c0, cw, False)
            rows_out(j).start()
            for side, cond in ((0, has_up), (1, has_down)):

                @pl.when(cond)
                def _():
                    edge_out(j, side).start()

    for outer, inner, make in pending:

        @when(outer, inner)
        def _():
            make().wait_send()

    @pl.when(first)
    def _():
        for side, cond in ((0, has_up), (1, has_down)):

            @pl.when(cond)
            def _():
                edge_in(side).wait_send()
                for j in range(len(chunks)):
                    edge_out(j, side).wait_send()

        for j in range(len(chunks)):
            rows_out(j).wait_send()

    @pl.when(jnp.logical_not(first))
    def _():
        for j in range(len(chunks)):
            rows_out(j).wait_recv()
        for side, cond in ((0, has_down), (1, has_up)):

            @pl.when(cond)
            def _():
                for j in range(len(chunks)):
                    edge_out(j, side).wait_recv()

        shift_rows()
        for b in range(width // WIDE):
            total = convolve(b, 0, WIDE)
            for block, bc, c0, cw, _ in chunks:
                if block == b:
                    finish(total[:, bc : bc + cw], c0, cw, True)


def in_kernel(activations, conv_weight, norm_gain, conv_bias):
    _, micros, rows, width = activations.shape
    taps, depth = conv_weight.shape[1:3]
    seqs = lax.axis_size("seq")
    shards = lax.axis_size("dp") * seqs
    count = len(column_chunks(width))
    dma = pltpu.SemaphoreType.DMA
    vmem = pl.BlockSpec(memory_space=pltpu.VMEM)
    anywhere = pl.BlockSpec(memory_space=pl.ANY)
    flops = 2 * micros * rows * taps * width * width
    return pl.pallas_call(
        functools.partial(kernel, seqs),
        out_shape=jax.ShapeDtypeStruct((1, 1, micros, rows, width), jnp.bfloat16),
        in_specs=[anywhere, anywhere, vmem, vmem],
        out_specs=vmem,
        scratch_shapes=[
            pltpu.VMEM((micros, rows, width), jnp.bfloat16),
            pltpu.VMEM((2, micros, EDGE, width), jnp.bfloat16),
            pltpu.VMEM((width // WIDE, taps, width, WIDE), jnp.bfloat16),
            pltpu.VMEM((micros, rows + 2 * EDGE, width), jnp.float32),
            pltpu.VMEM((micros * rows, taps * width), jnp.bfloat16),
            dma,
            dma((count,)),
            dma((count, 8 * seqs)),
            dma((count, shards)),
            dma((2,)),
            dma((2,)),
            dma((count,)),
            dma((count,)),
            dma((count, 2)),
            dma((count, 2)),
        ],
        cost_estimate=pl.CostEstimate(
            flops=flops, bytes_accessed=4 * activations.size, transcendentals=micros * rows * width
        ),
        compiler_params=pltpu.CompilerParams(
            collective_id=0, has_side_effects=True, vmem_limit_bytes=48 * 1024 * 1024
        ),
    )(activations, conv_weight, norm_gain, conv_bias)


def extended(cells, sides, width):
    for axis, dim in sides:
        count = lax.axis_size(axis)
        ends = count - 1
        head = lax.slice_in_dim(cells, 0, width, axis=dim)
        tail = lax.slice_in_dim(cells, cells.shape[dim] - width, cells.shape[dim], axis=dim)
        cells = jnp.concatenate(
            [
                lax.ppermute(tail, axis, [(i, (i + 1) % count) for i in range(ends)]),
                cells,
                lax.ppermute(head, axis, [((i + 1) % count, i) for i in range(ends)]),
            ],
            axis=dim,
        )
    return cells


def from_behind(block, axis, distance):
    devices = range(lax.axis_size(axis))
    route = [(i - distance, i) for i in devices if i - distance in devices]
    return lax.ppermute(block, axis, route)


def relayed(activations, conv_weight, norm_gain, conv_bias):
    kernel = lax.all_gather(conv_weight, ("dp", "seq"), axis=2, tiled=True)[0]
    gain = norm_gain[0]
    bias = conv_bias[0]
    inputs = activations[0]
    micro_count = inputs.shape[0]
    rows = inputs.shape[1]
    width = inputs.shape[2]
    segments = lax.axis_size("segment")
    segment = lax.axis_index("segment")
    turns = segments + micro_count - 1
    taps = kernel.shape[0]

    def convolve(padded):
        total = jnp.zeros((rows, width), jnp.float32)
        for tap in range(taps):
            total = total + jnp.dot(
                padded[tap : tap + rows], kernel[tap], preferred_element_type=jnp.float32
            )
        return total

    def skipped(padded):
        return jnp.zeros((rows, width), jnp.float32)

    def turn(step, carry):
        incoming, results, joined = carry
        micro = step - segment
        valid = jnp.logical_and(micro >= 0, micro < micro_count)
        picked = jnp.clip(micro, 0, micro_count - 1)
        own = lax.dynamic_index_in_dim(inputs, picked, 0, keepdims=False)
        current = jnp.where(segment == 0, own, incoming)
        wide = current.astype(jnp.float32)
        stat = jnp.mean(wide * wide, axis=-1, keepdims=True)
        normed = (wide / jnp.sqrt(stat + 1e-06) * gain).astype(jnp.bfloat16)
        padded = extended(normed, (("seq", 0),), 2)
        total = lax.cond(valid, convolve, skipped, padded)
        lifted = wide + jax.nn.gelu(total + bias, approximate=True)
        sent = lifted.astype(jnp.bfloat16)
        stored = lax.dynamic_update_index_in_dim(results, lifted, picked, 0)
        results = jnp.where(valid, stored, results)
        following = from_behind(sent, "segment", 1)
        return (following, results, joined)

    start = (
        jnp.zeros((rows, width), jnp.bfloat16),
        jnp.zeros((micro_count, rows, width), jnp.float32),
        jnp.zeros((micro_count, rows, width), jnp.bfloat16),
    )
    incoming, results, joined = lax.fori_loop(0, turns, turn, start)
    rounded = results.astype(jnp.bfloat16)
    joined = from_behind(rounded, "segment", segments - 1)
    final = (results + joined.astype(jnp.float32)).astype(jnp.bfloat16)
    output = jnp.where(segment == segments - 1, final, rounded)
    return output[None, None]


def per_device(activations, conv_weight, norm_gain, conv_bias):
    _, _, rows, width = activations.shape
    depth = conv_weight.shape[2]
    two_blocks = lax.axis_size("segment") == 2 and lax.axis_size("dp") == 4
    tiled = depth % EDGE == 0 and rows % EDGE == 0 and width % WIDE == 0
    fits = two_blocks and tiled and conv_weight.shape[1] // 2 <= EDGE and width > WIDE
    body = in_kernel if fits and lax.axis_size("seq") > 1 else relayed
    return body(activations, conv_weight, norm_gain, conv_bias)


def solution(mesh):
    in_specs = (
        P("dp", None, "seq", None),
        P("segment", None, ("dp", "seq"), None),
        P("segment", None),
        P("segment", None),
    )
    out_specs = P("segment", "dp", None, "seq", None)
    return jax.shard_map(
        per_device, mesh=mesh, in_specs=in_specs, out_specs=out_specs, check_vma=False
    )
```

```python
import functools

import jax
import jax.numpy as jnp
from jax import lax
from jax.experimental import pallas as pl
from jax.experimental.pallas import tpu as pltpu
from jax.sharding import PartitionSpec as P

EDGE = 16
HALF = 128
WIDE = 256


def column_chunks(width):
    return [(c // WIDE, c % WIDE, c, HALF) for c in range(0, width, HALF)]


def kernel(
    seqs, act, weight, gain_in, bias_in, out,
    gain, bias, xin, halo, wbuf, padded, shifted,
    load_sem, gain_sem, bias_sem, own_sem, wsend, wrecv, hsend, hrecv, rsend, rrecv, esend, erecv,
):
    micros, rows, width = xin.shape
    taps = weight.shape[1]
    depth = weight.shape[2]
    chunks = column_chunks(width)
    dp = lax.axis_index("dp")
    seg = lax.axis_index("segment")
    z = lax.axis_index("seq")
    chip, core = dp // 2, dp % 2
    sib = chip * 2 + (1 - core)
    across = (1 - chip) * 2 + core
    has_up = z + 1 < seqs
    has_down = z > 0
    first = seg == 0

    ring = [lax.rem(z + d, seqs) for d in range(seqs)]
    ways = seqs + 1

    barrier = pltpu.get_barrier_semaphore()

    def greet(device):
        pl.semaphore_signal(barrier, inc=1, device_id=device, device_id_type=pl.DeviceIdType.MESH)

    greet((sib, seg, z))
    greet((across, seg, z))
    greet((dp, 1 - seg, z))
    for at in ring[1:]:
        greet((dp, seg, at))

    @pl.when(has_up)
    def _():
        greet((dp, 1 - seg, z + 1))

    @pl.when(has_down)
    def _():
        greet((dp, 1 - seg, z - 1))

    own_w = []
    for j, (b, bc, c0, cw) in enumerate(chunks):
        start = pl.multiple_of((dp * seqs + z) * depth, EDGE)
        own_w.append(
            pltpu.make_async_copy(
                weight.at[0, :, :, pl.ds(c0, cw)],
                wbuf.at[b, :, pl.ds(start, depth), pl.ds(bc, cw)],
                own_sem.at[j],
            )
        )
        own_w[-1].start()
    load_x = pltpu.make_async_copy(act.at[0], xin, load_sem)
    load_gain = pltpu.make_async_copy(gain_in, gain, gain_sem)
    load_bias = pltpu.make_async_copy(bias_in, bias, bias_sem)
    load_gain.start()
    load_bias.start()

    @pl.when(first)
    def _():
        load_x.start()

    ends = jnp.int32(has_up) + jnp.int32(has_down)
    pl.semaphore_wait(barrier, 2 + seqs + ends)

    pending = []

    def piece(j, owner, at):
        b, bc, _, cw = chunks[j]
        start = pl.multiple_of((owner * seqs + at) * depth, EDGE)
        return wbuf.at[b, :, pl.ds(start, depth), pl.ds(bc, cw)]

    def transfer(j, owner, at, slot, way, own):
        c0, cw = chunks[j][2:4]
        dst = piece(j, owner, at)
        if way == 0:
            device = (sib, seg, z)
        elif way == 1:
            device = (across, seg, z)
        else:
            device = (dp, seg, ring[way - 1])
        return pltpu.make_async_remote_copy(
            src_ref=weight.at[0, :, :, pl.ds(c0, cw)] if own else dst,
            dst_ref=dst,
            send_sem=wsend.at[j, slot * ways + way],
            recv_sem=wrecv.at[j, owner * seqs + at],
            device_id=device,
            device_id_type=pl.DeviceIdType.MESH,
        )

    def send(*piece_and_way):
        transfer(*piece_and_way).start()
        pending.append(piece_and_way)

    def arrive(j, owner, at):
        transfer(j, owner, at, 0, 0, False).wait_recv()

    def send_own(j):
        for way in [*range(2, ways), 1, 0]:
            send(j, dp, z, 0, way, True)

    def from_column(j):
        for d in range(1, seqs):
            arrive(j, dp, ring[d])
            send(j, dp, ring[d], d, 1, False)
            send(j, dp, ring[d], d, 0, False)

    def from_across(j):
        for d in range(seqs):
            arrive(j, across, ring[d])
            send(j, across, ring[d], seqs + d, 0, False)

    def from_sibling(j):
        for at in ring:
            arrive(j, sib, at)
        for at in ring:
            arrive(j, (1 - chip) * 2 + (1 - core), at)

    def edge_in(side):
        up = side == 0
        return pltpu.make_async_remote_copy(
            src_ref=act.at[0, :, pl.ds(rows - EDGE if up else 0, EDGE), :],
            dst_ref=halo.at[side],
            send_sem=hsend.at[side],
            recv_sem=hrecv.at[side],
            device_id=(dp, seg, z + 1 if up else z - 1),
            device_id_type=pl.DeviceIdType.MESH,
        )

    def edge_out(j, side):
        up = side == 0
        cols = pl.ds(chunks[j][2], chunks[j][3])
        return pltpu.make_async_remote_copy(
            src_ref=out.at[0, 0, :, pl.ds(rows - EDGE if up else 0, EDGE), cols],
            dst_ref=halo.at[side, :, :, cols],
            send_sem=esend.at[j, side],
            recv_sem=erecv.at[j, side],
            device_id=(dp, 1 - seg, z + 1 if up else z - 1),
            device_id_type=pl.DeviceIdType.MESH,
        )

    def rows_out(j):
        cols = pl.ds(chunks[j][2], chunks[j][3])
        return pltpu.make_async_remote_copy(
            src_ref=out.at[0, 0, :, :, cols],
            dst_ref=xin.at[:, :, cols],
            send_sem=rsend.at[j],
            recv_sem=rrecv.at[j],
            device_id=(dp, 1 - seg, z),
            device_id_type=pl.DeviceIdType.MESH,
        )

    for side, cond in ((0, z == 0), (1, z == seqs - 1)):

        @pl.when(cond)
        def _():
            halo[side] = jnp.zeros(halo.shape[1:], halo.dtype)

    def normed(cells):
        wide = cells.astype(jnp.float32)
        stat = jnp.mean(wide * wide, axis=-1, keepdims=True)
        return wide * lax.rsqrt(stat + 1e-06) * gain[...]

    def shift_rows():
        def one(m, carry):
            padded[m, pl.ds(0, EDGE)] = normed(halo[0, m])
            padded[m, pl.ds(EDGE, rows)] = normed(xin[m])
            padded[m, pl.ds(EDGE + rows, EDGE)] = normed(halo[1, m])
            at = pl.multiple_of(m * rows, rows)
            for tap in range(taps):
                shifted[pl.ds(at, rows), pl.ds(tap * width, width)] = padded[
                    m, pl.ds(EDGE - taps // 2 + tap, rows), :
                ].astype(jnp.bfloat16)
            return carry

        lax.fori_loop(0, micros, one, 0)

    def convolve(b, bc, cw):
        kern = wbuf[b, :, :, pl.ds(bc, cw)].reshape(taps * width, cw)
        return jnp.dot(shifted[...], kern, preferred_element_type=jnp.float32)

    def finish(total, c0, cw, join):
        cols = pl.ds(c0, cw)
        wide = xin[:, :, cols].astype(jnp.float32)
        total = total.reshape(micros, rows, cw) + bias[:, cols].reshape(1, 1, cw)
        lifted = wide + jax.nn.gelu(total, approximate=True)
        if join:
            lifted = lifted + wide
        out[0, 0, :, :, cols] = lifted.astype(out.dtype)

    def complete(j):
        b, bc, c0, cw = chunks[j]
        from_across(j)
        from_sibling(j)

        @pl.when(first)
        def _():
            finish(convolve(b, bc, cw), c0, cw, False)
            rows_out(j).start()
            for side, cond in ((0, has_up), (1, has_down)):

                @pl.when(cond)
                def _():
                    edge_out(j, side).start()

    @pl.when(first)
    def _():
        for side, cond in ((0, has_up), (1, has_down)):

            @pl.when(cond)
            def _():
                edge_in(side).start()

    for j in range(len(chunks)):
        send_own(j)
    load_gain.wait()
    load_bias.wait()

    @pl.when(first)
    def _():
        load_x.wait()
        for side, cond in ((0, has_down), (1, has_up)):

            @pl.when(cond)
            def _():
                edge_in(side).wait_recv()

        shift_rows()

    for copy in own_w:
        copy.wait()
    for j in range(len(chunks)):
        from_column(j)
        if j > 0:
            complete(j - 1)
    complete(len(chunks) - 1)

    for piece_and_way in pending:
        transfer(*piece_and_way).wait_send()

    @pl.when(first)
    def _():
        for side, cond in ((0, has_up), (1, has_down)):

            @pl.when(cond)
            def _():
                edge_in(side).wait_send()
                for j in range(len(chunks)):
                    edge_out(j, side).wait_send()

        for j in range(len(chunks)):
            rows_out(j).wait_send()

    @pl.when(jnp.logical_not(first))
    def _():
        for j in range(len(chunks)):
            rows_out(j).wait_recv()
        for side, cond in ((0, has_down), (1, has_up)):

            @pl.when(cond)
            def _():
                for j in range(len(chunks)):
                    edge_out(j, side).wait_recv()

        shift_rows()
        for b in range(width // WIDE):
            total = convolve(b, 0, WIDE)
            for block, bc, c0, cw in chunks:
                if block == b:
                    finish(total[:, bc : bc + cw], c0, cw, True)


def in_kernel(activations, conv_weight, norm_gain, conv_bias):
    _, micros, rows, width = activations.shape
    taps, depth = conv_weight.shape[1:3]
    seqs = lax.axis_size("seq")
    shards = lax.axis_size("dp") * seqs
    count = len(column_chunks(width))
    dma = pltpu.SemaphoreType.DMA
    vmem = pl.BlockSpec(memory_space=pltpu.VMEM)
    anywhere = pl.BlockSpec(memory_space=pl.ANY)
    flops = 2 * micros * rows * taps * width * width
    return pl.pallas_call(
        functools.partial(kernel, seqs),
        out_shape=jax.ShapeDtypeStruct((1, 1, micros, rows, width), jnp.bfloat16),
        in_specs=[anywhere] * 4,
        out_specs=vmem,
        scratch_shapes=[
            pltpu.VMEM((1, width), jnp.float32),
            pltpu.VMEM((1, width), jnp.float32),
            pltpu.VMEM((micros, rows, width), jnp.bfloat16),
            pltpu.VMEM((2, micros, EDGE, width), jnp.bfloat16),
            pltpu.VMEM((width // WIDE, taps, width, WIDE), jnp.bfloat16),
            pltpu.VMEM((micros, rows + 2 * EDGE, width), jnp.float32),
            pltpu.VMEM((micros * rows, taps * width), jnp.bfloat16),
            dma,
            dma,
            dma,
            dma((count,)),
            dma((count, 2 * seqs * (seqs + 1))),
            dma((count, shards)),
            dma((2,)),
            dma((2,)),
            dma((count,)),
            dma((count,)),
            dma((count, 2)),
            dma((count, 2)),
        ],
        cost_estimate=pl.CostEstimate(
            flops=flops, bytes_accessed=4 * activations.size, transcendentals=micros * rows * width
        ),
        compiler_params=pltpu.CompilerParams(
            collective_id=0, has_side_effects=True, vmem_limit_bytes=60 * 1024 * 1024
        ),
    )(activations, conv_weight, norm_gain, conv_bias)


def extended(cells, sides, width):
    for axis, dim in sides:
        count = lax.axis_size(axis)
        ends = count - 1
        head = lax.slice_in_dim(cells, 0, width, axis=dim)
        tail = lax.slice_in_dim(cells, cells.shape[dim] - width, cells.shape[dim], axis=dim)
        cells = jnp.concatenate(
            [
                lax.ppermute(tail, axis, [(i, (i + 1) % count) for i in range(ends)]),
                cells,
                lax.ppermute(head, axis, [((i + 1) % count, i) for i in range(ends)]),
            ],
            axis=dim,
        )
    return cells


def from_behind(block, axis, distance):
    devices = range(lax.axis_size(axis))
    route = [(i - distance, i) for i in devices if i - distance in devices]
    return lax.ppermute(block, axis, route)


def relayed(activations, conv_weight, norm_gain, conv_bias):
    kernel = lax.all_gather(conv_weight, ("dp", "seq"), axis=2, tiled=True)[0]
    gain = norm_gain[0]
    bias = conv_bias[0]
    inputs = activations[0]
    micro_count = inputs.shape[0]
    rows = inputs.shape[1]
    width = inputs.shape[2]
    segments = lax.axis_size("segment")
    segment = lax.axis_index("segment")
    turns = segments + micro_count - 1
    taps = kernel.shape[0]

    def convolve(padded):
        total = jnp.zeros((rows, width), jnp.float32)
        for tap in range(taps):
            total = total + jnp.dot(
                padded[tap : tap + rows], kernel[tap], preferred_element_type=jnp.float32
            )
        return total

    def skipped(padded):
        return jnp.zeros((rows, width), jnp.float32)

    def turn(step, carry):
        incoming, results, joined = carry
        micro = step - segment
        valid = jnp.logical_and(micro >= 0, micro < micro_count)
        picked = jnp.clip(micro, 0, micro_count - 1)
        own = lax.dynamic_index_in_dim(inputs, picked, 0, keepdims=False)
        current = jnp.where(segment == 0, own, incoming)
        wide = current.astype(jnp.float32)
        stat = jnp.mean(wide * wide, axis=-1, keepdims=True)
        normed = (wide / jnp.sqrt(stat + 1e-06) * gain).astype(jnp.bfloat16)
        padded = extended(normed, (("seq", 0),), 2)
        total = lax.cond(valid, convolve, skipped, padded)
        lifted = wide + jax.nn.gelu(total + bias, approximate=True)
        sent = lifted.astype(jnp.bfloat16)
        stored = lax.dynamic_update_index_in_dim(results, lifted, picked, 0)
        results = jnp.where(valid, stored, results)
        following = from_behind(sent, "segment", 1)
        return (following, results, joined)

    start = (
        jnp.zeros((rows, width), jnp.bfloat16),
        jnp.zeros((micro_count, rows, width), jnp.float32),
        jnp.zeros((micro_count, rows, width), jnp.bfloat16),
    )
    incoming, results, joined = lax.fori_loop(0, turns, turn, start)
    rounded = results.astype(jnp.bfloat16)
    joined = from_behind(rounded, "segment", segments - 1)
    final = (results + joined.astype(jnp.float32)).astype(jnp.bfloat16)
    output = jnp.where(segment == segments - 1, final, rounded)
    return output[None, None]


def per_device(activations, conv_weight, norm_gain, conv_bias):
    _, _, rows, width = activations.shape
    depth = conv_weight.shape[2]
    two_blocks = lax.axis_size("segment") == 2 and lax.axis_size("dp") == 4
    tiled = depth % EDGE == 0 and rows % EDGE == 0 and width % WIDE == 0
    fits = two_blocks and tiled and conv_weight.shape[1] // 2 <= EDGE and width > WIDE
    body = in_kernel if fits and lax.axis_size("seq") > 1 else relayed
    return body(activations, conv_weight, norm_gain, conv_bias)


def solution(mesh):
    in_specs = (
        P("dp", None, "seq", None),
        P("segment", None, ("dp", "seq"), None),
        P("segment", None),
        P("segment", None),
    )
    out_specs = P("segment", "dp", None, "seq", None)
    return jax.shard_map(
        per_device, mesh=mesh, in_specs=in_specs, out_specs=out_specs, check_vma=False
    )
```

```python
import functools

import jax
import jax.numpy as jnp
from jax import lax
from jax.experimental import pallas as pl
from jax.experimental.pallas import tpu as pltpu
from jax.sharding import PartitionSpec as P

EDGE = 16
HALF = 128
WIDE = 256


def kernel(
    seqs, act, weight, gain_in, bias_in, out,
    gain, bias, xin, halo, wbuf, padded, shifted,
    load_sem, gain_sem, bias_sem, own_sem, wsend, wrecv, hsend, hrecv, rsend, rrecv, esend, erecv,
):
    micros, rows, width = xin.shape
    taps = weight.shape[1]
    count = width // HALF
    dp = lax.axis_index("dp")
    seg = lax.axis_index("segment")
    z = lax.axis_index("seq")
    chip, core = dp // 2, dp % 2
    sib = chip * 2 + (1 - core)
    across = (1 - chip) * 2 + core
    has_up = z + 1 < seqs
    has_down = z > 0
    first = seg == 0

    ring = [lax.rem(z + d, seqs) for d in range(seqs)]
    ways = seqs + 1

    barrier = pltpu.get_barrier_semaphore()

    def greet(device):
        pl.semaphore_signal(barrier, inc=1, device_id=device, device_id_type=pl.DeviceIdType.MESH)

    greet((sib, seg, z))
    greet((across, seg, z))
    greet((dp, 1 - seg, z))
    for at in ring[1:]:
        greet((dp, seg, at))

    @pl.when(has_up)
    def _():
        greet((dp, 1 - seg, z + 1))

    @pl.when(has_down)
    def _():
        greet((dp, 1 - seg, z - 1))

    def piece(j, owner, at):
        return wbuf.at[j, owner * seqs + at]

    own_w = []
    for j in range(count):
        own_w.append(
            pltpu.make_async_copy(
                weight.at[0, :, :, pl.ds(j * HALF, HALF)], piece(j, dp, z), own_sem.at[j]
            )
        )
        own_w[-1].start()
    load_x = pltpu.make_async_copy(act.at[0], xin, load_sem)
    load_gain = pltpu.make_async_copy(gain_in, gain, gain_sem)
    load_bias = pltpu.make_async_copy(bias_in, bias, bias_sem)
    load_gain.start()
    load_bias.start()

    @pl.when(first)
    def _():
        load_x.start()

    ends = jnp.int32(has_up) + jnp.int32(has_down)
    pl.semaphore_wait(barrier, 2 + seqs + ends)

    pending = []

    def transfer(j, owner, at, slot, way):
        block = piece(j, owner, at)
        if way == 0:
            device = (sib, seg, z)
        elif way == 1:
            device = (across, seg, z)
        else:
            device = (dp, seg, ring[way - 1])
        return pltpu.make_async_remote_copy(
            src_ref=block,
            dst_ref=block,
            send_sem=wsend.at[j, slot * ways + way],
            recv_sem=wrecv.at[j, owner * seqs + at],
            device_id=device,
            device_id_type=pl.DeviceIdType.MESH,
        )

    def send(*piece_and_way):
        transfer(*piece_and_way).start()
        pending.append(piece_and_way)

    def arrive(j, owner, at):
        transfer(j, owner, at, 0, 0).wait_recv()

    def send_own(j):
        for way in [*range(2, ways), 1, 0]:
            send(j, dp, z, 0, way)

    def from_column(j):
        for d in range(1, seqs):
            arrive(j, dp, ring[d])
            send(j, dp, ring[d], d, 1)
            send(j, dp, ring[d], d, 0)

    def from_across(j):
        for d in range(seqs):
            arrive(j, across, ring[d])
            send(j, across, ring[d], seqs + d, 0)

    def from_sibling(j):
        for at in ring:
            arrive(j, sib, at)
        for at in ring:
            arrive(j, (1 - chip) * 2 + (1 - core), at)

    def edge_in(side):
        up = side == 0
        return pltpu.make_async_remote_copy(
            src_ref=act.at[0, :, pl.ds(rows - EDGE if up else 0, EDGE), :],
            dst_ref=halo.at[side],
            send_sem=hsend.at[side],
            recv_sem=hrecv.at[side],
            device_id=(dp, seg, z + 1 if up else z - 1),
            device_id_type=pl.DeviceIdType.MESH,
        )

    def edge_out(j, side):
        up = side == 0
        cols = pl.ds(j * HALF, HALF)
        return pltpu.make_async_remote_copy(
            src_ref=out.at[0, 0, :, pl.ds(rows - EDGE if up else 0, EDGE), cols],
            dst_ref=halo.at[side, :, :, cols],
            send_sem=esend.at[j, side],
            recv_sem=erecv.at[j, side],
            device_id=(dp, 1 - seg, z + 1 if up else z - 1),
            device_id_type=pl.DeviceIdType.MESH,
        )

    def rows_out(j):
        cols = pl.ds(j * HALF, HALF)
        return pltpu.make_async_remote_copy(
            src_ref=out.at[0, 0, :, :, cols],
            dst_ref=xin.at[:, :, cols],
            send_sem=rsend.at[j],
            recv_sem=rrecv.at[j],
            device_id=(dp, 1 - seg, z),
            device_id_type=pl.DeviceIdType.MESH,
        )

    for side, cond in ((0, z == 0), (1, z == seqs - 1)):

        @pl.when(cond)
        def _():
            halo[side] = jnp.zeros(halo.shape[1:], halo.dtype)

    def normed(cells):
        wide = cells.astype(jnp.float32)
        stat = jnp.mean(wide * wide, axis=-1, keepdims=True)
        return wide * lax.rsqrt(stat + 1e-06) * gain[...]

    def shift_rows():
        def one(m, carry):
            padded[m, pl.ds(0, EDGE)] = normed(halo[0, m])
            padded[m, pl.ds(EDGE, rows)] = normed(xin[m])
            padded[m, pl.ds(EDGE + rows, EDGE)] = normed(halo[1, m])
            at = pl.multiple_of(m * rows, rows)
            for tap in range(taps):
                shifted[pl.ds(at, rows), pl.ds(tap * width, width)] = padded[
                    m, pl.ds(EDGE - taps // 2 + tap, rows), :
                ].astype(jnp.bfloat16)
            return carry

        lax.fori_loop(0, micros, one, 0)

    def convolve(*parts):
        kern = jnp.concatenate(
            [
                jnp.concatenate([wbuf[j, :, tap].reshape(width, HALF) for j in parts], axis=1)
                for tap in range(taps)
            ],
            axis=0,
        )
        return jnp.dot(shifted[...], kern, preferred_element_type=jnp.float32)

    def finish(total, c0, cw, join):
        cols = pl.ds(c0, cw)
        wide = xin[:, :, cols].astype(jnp.float32)
        total = total.reshape(micros, rows, cw) + bias[:, cols].reshape(1, 1, cw)
        lifted = wide + jax.nn.gelu(total, approximate=True)
        if join:
            lifted = lifted + wide
        out[0, 0, :, :, cols] = lifted.astype(out.dtype)

    def complete(j):
        from_across(j)
        from_sibling(j)

        @pl.when(first)
        def _():
            finish(convolve(j), j * HALF, HALF, False)
            rows_out(j).start()
            for side, cond in ((0, has_up), (1, has_down)):

                @pl.when(cond)
                def _():
                    edge_out(j, side).start()

    @pl.when(first)
    def _():
        for side, cond in ((0, has_up), (1, has_down)):

            @pl.when(cond)
            def _():
                edge_in(side).start()

    for j in range(count):
        own_w[j].wait()
        send_own(j)
    load_gain.wait()
    load_bias.wait()

    @pl.when(first)
    def _():
        load_x.wait()
        for side, cond in ((0, has_down), (1, has_up)):

            @pl.when(cond)
            def _():
                edge_in(side).wait_recv()

        shift_rows()

    for j in range(count):
        from_column(j)
        if j > 0:
            complete(j - 1)
    complete(count - 1)

    for piece_and_way in pending:
        transfer(*piece_and_way).wait_send()

    @pl.when(first)
    def _():
        for side, cond in ((0, has_up), (1, has_down)):

            @pl.when(cond)
            def _():
                edge_in(side).wait_send()
                for j in range(count):
                    edge_out(j, side).wait_send()

        for j in range(count):
            rows_out(j).wait_send()

    @pl.when(jnp.logical_not(first))
    def _():
        for j in range(count):
            rows_out(j).wait_recv()
        for side, cond in ((0, has_down), (1, has_up)):

            @pl.when(cond)
            def _():
                for j in range(count):
                    edge_out(j, side).wait_recv()

        shift_rows()
        for j in range(0, count, 2):
            finish(convolve(j, j + 1), j * HALF, WIDE, True)


def in_kernel(activations, conv_weight, norm_gain, conv_bias):
    _, micros, rows, width = activations.shape
    taps, depth = conv_weight.shape[1:3]
    seqs = lax.axis_size("seq")
    shards = lax.axis_size("dp") * seqs
    count = width // HALF
    dma = pltpu.SemaphoreType.DMA
    vmem = pl.BlockSpec(memory_space=pltpu.VMEM)
    anywhere = pl.BlockSpec(memory_space=pl.ANY)
    flops = 2 * micros * rows * taps * width * width
    return pl.pallas_call(
        functools.partial(kernel, seqs),
        out_shape=jax.ShapeDtypeStruct((1, 1, micros, rows, width), jnp.bfloat16),
        in_specs=[anywhere] * 4,
        out_specs=vmem,
        scratch_shapes=[
            pltpu.VMEM((1, width), jnp.float32),
            pltpu.VMEM((1, width), jnp.float32),
            pltpu.VMEM((micros, rows, width), jnp.bfloat16),
            pltpu.VMEM((2, micros, EDGE, width), jnp.bfloat16),
            pltpu.VMEM((count, shards, taps, depth, HALF), jnp.bfloat16),
            pltpu.VMEM((micros, rows + 2 * EDGE, width), jnp.float32),
            pltpu.VMEM((micros * rows, taps * width), jnp.bfloat16),
            dma,
            dma,
            dma,
            dma((count,)),
            dma((count, 2 * seqs * (seqs + 1))),
            dma((count, shards)),
            dma((2,)),
            dma((2,)),
            dma((count,)),
            dma((count,)),
            dma((count, 2)),
            dma((count, 2)),
        ],
        cost_estimate=pl.CostEstimate(
            flops=flops, bytes_accessed=4 * activations.size, transcendentals=micros * rows * width
        ),
        compiler_params=pltpu.CompilerParams(
            collective_id=0, has_side_effects=True, vmem_limit_bytes=60 * 1024 * 1024
        ),
    )(activations, conv_weight, norm_gain, conv_bias)


def extended(cells, sides, width):
    for axis, dim in sides:
        count = lax.axis_size(axis)
        ends = count - 1
        head = lax.slice_in_dim(cells, 0, width, axis=dim)
        tail = lax.slice_in_dim(cells, cells.shape[dim] - width, cells.shape[dim], axis=dim)
        cells = jnp.concatenate(
            [
                lax.ppermute(tail, axis, [(i, (i + 1) % count) for i in range(ends)]),
                cells,
                lax.ppermute(head, axis, [((i + 1) % count, i) for i in range(ends)]),
            ],
            axis=dim,
        )
    return cells


def from_behind(block, axis, distance):
    devices = range(lax.axis_size(axis))
    route = [(i - distance, i) for i in devices if i - distance in devices]
    return lax.ppermute(block, axis, route)


def relayed(activations, conv_weight, norm_gain, conv_bias):
    kernel = lax.all_gather(conv_weight, ("dp", "seq"), axis=2, tiled=True)[0]
    gain = norm_gain[0]
    bias = conv_bias[0]
    inputs = activations[0]
    micro_count = inputs.shape[0]
    rows = inputs.shape[1]
    width = inputs.shape[2]
    segments = lax.axis_size("segment")
    segment = lax.axis_index("segment")
    turns = segments + micro_count - 1
    taps = kernel.shape[0]

    def convolve(padded):
        total = jnp.zeros((rows, width), jnp.float32)
        for tap in range(taps):
            total = total + jnp.dot(
                padded[tap : tap + rows], kernel[tap], preferred_element_type=jnp.float32
            )
        return total

    def skipped(padded):
        return jnp.zeros((rows, width), jnp.float32)

    def turn(step, carry):
        incoming, results, joined = carry
        micro = step - segment
        valid = jnp.logical_and(micro >= 0, micro < micro_count)
        picked = jnp.clip(micro, 0, micro_count - 1)
        own = lax.dynamic_index_in_dim(inputs, picked, 0, keepdims=False)
        current = jnp.where(segment == 0, own, incoming)
        wide = current.astype(jnp.float32)
        stat = jnp.mean(wide * wide, axis=-1, keepdims=True)
        normed = (wide / jnp.sqrt(stat + 1e-06) * gain).astype(jnp.bfloat16)
        padded = extended(normed, (("seq", 0),), 2)
        total = lax.cond(valid, convolve, skipped, padded)
        lifted = wide + jax.nn.gelu(total + bias, approximate=True)
        sent = lifted.astype(jnp.bfloat16)
        stored = lax.dynamic_update_index_in_dim(results, lifted, picked, 0)
        results = jnp.where(valid, stored, results)
        following = from_behind(sent, "segment", 1)
        return (following, results, joined)

    start = (
        jnp.zeros((rows, width), jnp.bfloat16),
        jnp.zeros((micro_count, rows, width), jnp.float32),
        jnp.zeros((micro_count, rows, width), jnp.bfloat16),
    )
    incoming, results, joined = lax.fori_loop(0, turns, turn, start)
    rounded = results.astype(jnp.bfloat16)
    joined = from_behind(rounded, "segment", segments - 1)
    final = (results + joined.astype(jnp.float32)).astype(jnp.bfloat16)
    output = jnp.where(segment == segments - 1, final, rounded)
    return output[None, None]


def per_device(activations, conv_weight, norm_gain, conv_bias):
    _, _, rows, width = activations.shape
    depth = conv_weight.shape[2]
    two_blocks = lax.axis_size("segment") == 2 and lax.axis_size("dp") == 4
    tiled = depth % EDGE == 0 and rows % EDGE == 0 and width % WIDE == 0
    fits = two_blocks and tiled and conv_weight.shape[1] // 2 <= EDGE and width > WIDE
    body = in_kernel if fits and lax.axis_size("seq") > 1 else relayed
    return body(activations, conv_weight, norm_gain, conv_bias)


def solution(mesh):
    in_specs = (
        P("dp", None, "seq", None),
        P("segment", None, ("dp", "seq"), None),
        P("segment", None),
        P("segment", None),
    )
    out_specs = P("segment", "dp", None, "seq", None)
    return jax.shard_map(
        per_device, mesh=mesh, in_specs=in_specs, out_specs=out_specs, check_vma=False
    )
```

```python
import functools

import jax
import jax.numpy as jnp
from jax import lax
from jax.experimental import pallas as pl
from jax.experimental.pallas import tpu as pltpu
from jax.sharding import PartitionSpec as P

EDGE = 16
HALF = 128
WIDE = 256


def kernel(
    seqs, act, weight, gain_in, bias_in, out,
    gain, bias, xin, halo, wbuf, padded, shifted,
    load_sem, gain_sem, bias_sem, own_sem, wsend, wrecv, hsend, hrecv, rsend, rrecv, esend, erecv,
):
    micros, rows, width = xin.shape
    taps = weight.shape[1]
    count = width // HALF
    dp = lax.axis_index("dp")
    seg = lax.axis_index("segment")
    z = lax.axis_index("seq")
    chip, core = dp // 2, dp % 2
    sib = chip * 2 + (1 - core)
    across = (1 - chip) * 2 + core
    has_up = z + 1 < seqs
    has_down = z > 0
    first = seg == 0

    ring = [lax.rem(z + d, seqs) for d in range(seqs)]
    ways = seqs + 2

    barrier = pltpu.get_barrier_semaphore()

    def greet(device):
        pl.semaphore_signal(barrier, inc=1, device_id=device, device_id_type=pl.DeviceIdType.MESH)

    greet((sib, seg, z))
    greet((across, seg, z))
    greet((dp, 1 - seg, z))
    for at in ring[1:]:
        greet((dp, seg, at))

    @pl.when(has_up)
    def _():
        greet((dp, 1 - seg, z + 1))

    @pl.when(has_down)
    def _():
        greet((dp, 1 - seg, z - 1))

    def piece(j, owner, at):
        return wbuf.at[j, owner * seqs + at]

    own_w = []
    for j in range(count):
        own_w.append(
            pltpu.make_async_copy(
                weight.at[0, :, :, pl.ds(j * HALF, HALF)], piece(j, dp, z), own_sem.at[j]
            )
        )
        own_w[-1].start()
    load_x = pltpu.make_async_copy(act.at[0], xin, load_sem)
    load_gain = pltpu.make_async_copy(gain_in, gain, gain_sem)
    load_bias = pltpu.make_async_copy(bias_in, bias, bias_sem)
    load_gain.start()
    load_bias.start()

    @pl.when(first)
    def _():
        load_x.start()

    ends = jnp.int32(has_up) + jnp.int32(has_down)
    pl.semaphore_wait(barrier, 2 + seqs + ends)

    pending = []

    def transfer(j, owner, at, slot, way, to=None):
        block = piece(j, owner, at)
        if way == 0:
            device = (sib, seg, z)
        elif way == 1:
            device = (across, seg, z)
        else:
            device = (dp, seg, to)
        return pltpu.make_async_remote_copy(
            src_ref=block,
            dst_ref=block,
            send_sem=wsend.at[j, slot * ways + way],
            recv_sem=wrecv.at[j, owner * seqs + at],
            device_id=device,
            device_id_type=pl.DeviceIdType.MESH,
        )

    def send(cond, *transfer_args):
        if cond is None:
            transfer(*transfer_args).start()
        else:

            @pl.when(cond)
            def _():
                transfer(*transfer_args).start()

        pending.append((cond, transfer_args))

    def arrive(j, owner, at):
        transfer(j, owner, at, 0, 0).wait_recv()

    last = seqs - 1
    near = [jnp.logical_or(t == z + 1, t == z - 1) for t in ring]
    direct = [
        jnp.logical_or(near[d], jnp.logical_and(ring[d] > 0, ring[d] < last)) for d in range(seqs)
    ]
    to_first = [jnp.logical_and(z == 1, t > z) for t in ring]
    to_last = [jnp.logical_and(z == last - 1, t < z) for t in ring]
    partner = z + 1 - 2 * (z % 2)
    not_partner = [t != partner for t in ring]

    def by_partner(j):
        return seqs % 2 == 0 and j % 2 == 0

    def send_own(j):
        for d in range(1, seqs):
            send(direct[d], j, dp, z, 0, 1 + d, ring[d])
        send(None, j, dp, z, 0, 1)
        send(None, j, dp, z, 0, 0)

    def from_column(j):
        arrive(j, across, z)
        if by_partner(j):
            send(None, j, across, z, seqs, 2, partner)
        send(None, j, across, z, seqs, 0)
        for d in [1, *range(seqs - 1, 1, -1)]:
            arrive(j, dp, ring[d])
            send(to_first[d], j, dp, ring[d], d, 2, z - 1)
            send(to_last[d], j, dp, ring[d], d, 3, z + 1)
            send(not_partner[d] if by_partner(j) else None, j, dp, ring[d], d, 1)
            send(None, j, dp, ring[d], d, 0)

    def from_across(j):
        for d in range(1, seqs):
            arrive(j, across, ring[d])
            send(None, j, across, ring[d], seqs + d, 0)

    def from_sibling(j):
        for at in ring:
            arrive(j, sib, at)
        for at in ring:
            arrive(j, (1 - chip) * 2 + (1 - core), at)

    def edge_in(side):
        up = side == 0
        return pltpu.make_async_remote_copy(
            src_ref=act.at[0, :, pl.ds(rows - EDGE if up else 0, EDGE), :],
            dst_ref=halo.at[side],
            send_sem=hsend.at[side],
            recv_sem=hrecv.at[side],
            device_id=(dp, seg, z + 1 if up else z - 1),
            device_id_type=pl.DeviceIdType.MESH,
        )

    def edge_out(j, side):
        up = side == 0
        cols = pl.ds(j * HALF, HALF)
        return pltpu.make_async_remote_copy(
            src_ref=out.at[0, 0, :, pl.ds(rows - EDGE if up else 0, EDGE), cols],
            dst_ref=halo.at[side, :, :, cols],
            send_sem=esend.at[j, side],
            recv_sem=erecv.at[j, side],
            device_id=(dp, 1 - seg, z + 1 if up else z - 1),
            device_id_type=pl.DeviceIdType.MESH,
        )

    def rows_out(j):
        cols = pl.ds(j * HALF, HALF)
        return pltpu.make_async_remote_copy(
            src_ref=out.at[0, 0, :, :, cols],
            dst_ref=xin.at[:, :, cols],
            send_sem=rsend.at[j],
            recv_sem=rrecv.at[j],
            device_id=(dp, 1 - seg, z),
            device_id_type=pl.DeviceIdType.MESH,
        )

    for side, cond in ((0, z == 0), (1, z == seqs - 1)):

        @pl.when(cond)
        def _():
            halo[side] = jnp.zeros(halo.shape[1:], halo.dtype)

    def normed(cells):
        wide = cells.astype(jnp.float32)
        stat = jnp.mean(wide * wide, axis=-1, keepdims=True)
        return wide * lax.rsqrt(stat + 1e-06) * gain[...]

    def shift_rows():
        def one(m, carry):
            padded[m, pl.ds(0, EDGE)] = normed(halo[0, m])
            padded[m, pl.ds(EDGE, rows)] = normed(xin[m])
            padded[m, pl.ds(EDGE + rows, EDGE)] = normed(halo[1, m])
            at = pl.multiple_of(m * rows, rows)
            for tap in range(taps):
                shifted[pl.ds(at, rows), pl.ds(tap * width, width)] = padded[
                    m, pl.ds(EDGE - taps // 2 + tap, rows), :
                ].astype(jnp.bfloat16)
            return carry

        lax.fori_loop(0, micros, one, 0)

    def convolve(*parts):
        kern = jnp.concatenate(
            [
                jnp.concatenate([wbuf[j, :, tap].reshape(width, HALF) for j in parts], axis=1)
                for tap in range(taps)
            ],
            axis=0,
        )
        return jnp.dot(shifted[...], kern, preferred_element_type=jnp.float32)

    def finish(total, c0, cw, join):
        cols = pl.ds(c0, cw)
        wide = xin[:, :, cols].astype(jnp.float32)
        total = total.reshape(micros, rows, cw) + bias[:, cols].reshape(1, 1, cw)
        lifted = wide + jax.nn.gelu(total, approximate=True)
        if join:
            lifted = lifted + wide
        out[0, 0, :, :, cols] = lifted.astype(out.dtype)

    def complete(j):
        from_across(j)
        from_sibling(j)

        @pl.when(first)
        def _():
            finish(convolve(j), j * HALF, HALF, False)
            rows_out(j).start()
            for side, cond in ((0, has_up), (1, has_down)):

                @pl.when(cond)
                def _():
                    edge_out(j, side).start()

    @pl.when(first)
    def _():
        for side, cond in ((0, has_up), (1, has_down)):

            @pl.when(cond)
            def _():
                edge_in(side).start()

    for j in range(count):
        own_w[j].wait()
        send_own(j)
    load_gain.wait()
    load_bias.wait()

    @pl.when(first)
    def _():
        load_x.wait()
        for side, cond in ((0, has_down), (1, has_up)):

            @pl.when(cond)
            def _():
                edge_in(side).wait_recv()

        shift_rows()

    for j in range(count):
        from_column(j)
        if j > 0:
            complete(j - 1)
    complete(count - 1)

    for cond, transfer_args in pending:
        if cond is None:
            transfer(*transfer_args).wait_send()
        else:

            @pl.when(cond)
            def _():
                transfer(*transfer_args).wait_send()

    @pl.when(first)
    def _():
        for side, cond in ((0, has_up), (1, has_down)):

            @pl.when(cond)
            def _():
                edge_in(side).wait_send()
                for j in range(count):
                    edge_out(j, side).wait_send()

        for j in range(count):
            rows_out(j).wait_send()

    @pl.when(jnp.logical_not(first))
    def _():
        for j in range(count):
            rows_out(j).wait_recv()
        for side, cond in ((0, has_down), (1, has_up)):

            @pl.when(cond)
            def _():
                for j in range(count):
                    edge_out(j, side).wait_recv()

        shift_rows()
        for j in range(0, count, 2):
            finish(convolve(j, j + 1), j * HALF, WIDE, True)


def in_kernel(activations, conv_weight, norm_gain, conv_bias):
    _, micros, rows, width = activations.shape
    taps, depth = conv_weight.shape[1:3]
    seqs = lax.axis_size("seq")
    shards = lax.axis_size("dp") * seqs
    count = width // HALF
    dma = pltpu.SemaphoreType.DMA
    vmem = pl.BlockSpec(memory_space=pltpu.VMEM)
    anywhere = pl.BlockSpec(memory_space=pl.ANY)
    flops = 2 * micros * rows * taps * width * width
    return pl.pallas_call(
        functools.partial(kernel, seqs),
        out_shape=jax.ShapeDtypeStruct((1, 1, micros, rows, width), jnp.bfloat16),
        in_specs=[anywhere] * 4,
        out_specs=vmem,
        scratch_shapes=[
            pltpu.VMEM((1, width), jnp.float32),
            pltpu.VMEM((1, width), jnp.float32),
            pltpu.VMEM((micros, rows, width), jnp.bfloat16),
            pltpu.VMEM((2, micros, EDGE, width), jnp.bfloat16),
            pltpu.VMEM((count, shards, taps, depth, HALF), jnp.bfloat16),
            pltpu.VMEM((micros, rows + 2 * EDGE, width), jnp.float32),
            pltpu.VMEM((micros * rows, taps * width), jnp.bfloat16),
            dma,
            dma,
            dma,
            dma((count,)),
            dma((count, 2 * seqs * (seqs + 2))),
            dma((count, shards)),
            dma((2,)),
            dma((2,)),
            dma((count,)),
            dma((count,)),
            dma((count, 2)),
            dma((count, 2)),
        ],
        cost_estimate=pl.CostEstimate(
            flops=flops, bytes_accessed=4 * activations.size, transcendentals=micros * rows * width
        ),
        compiler_params=pltpu.CompilerParams(
            collective_id=0, has_side_effects=True, vmem_limit_bytes=60 * 1024 * 1024
        ),
    )(activations, conv_weight, norm_gain, conv_bias)


def extended(cells, sides, width):
    for axis, dim in sides:
        count = lax.axis_size(axis)
        ends = count - 1
        head = lax.slice_in_dim(cells, 0, width, axis=dim)
        tail = lax.slice_in_dim(cells, cells.shape[dim] - width, cells.shape[dim], axis=dim)
        cells = jnp.concatenate(
            [
                lax.ppermute(tail, axis, [(i, (i + 1) % count) for i in range(ends)]),
                cells,
                lax.ppermute(head, axis, [((i + 1) % count, i) for i in range(ends)]),
            ],
            axis=dim,
        )
    return cells


def from_behind(block, axis, distance):
    devices = range(lax.axis_size(axis))
    route = [(i - distance, i) for i in devices if i - distance in devices]
    return lax.ppermute(block, axis, route)


def relayed(activations, conv_weight, norm_gain, conv_bias):
    kernel = lax.all_gather(conv_weight, ("dp", "seq"), axis=2, tiled=True)[0]
    gain = norm_gain[0]
    bias = conv_bias[0]
    inputs = activations[0]
    micro_count = inputs.shape[0]
    rows = inputs.shape[1]
    width = inputs.shape[2]
    segments = lax.axis_size("segment")
    segment = lax.axis_index("segment")
    turns = segments + micro_count - 1
    taps = kernel.shape[0]

    def convolve(padded):
        total = jnp.zeros((rows, width), jnp.float32)
        for tap in range(taps):
            total = total + jnp.dot(
                padded[tap : tap + rows], kernel[tap], preferred_element_type=jnp.float32
            )
        return total

    def skipped(padded):
        return jnp.zeros((rows, width), jnp.float32)

    def turn(step, carry):
        incoming, results, joined = carry
        micro = step - segment
        valid = jnp.logical_and(micro >= 0, micro < micro_count)
        picked = jnp.clip(micro, 0, micro_count - 1)
        own = lax.dynamic_index_in_dim(inputs, picked, 0, keepdims=False)
        current = jnp.where(segment == 0, own, incoming)
        wide = current.astype(jnp.float32)
        stat = jnp.mean(wide * wide, axis=-1, keepdims=True)
        normed = (wide / jnp.sqrt(stat + 1e-06) * gain).astype(jnp.bfloat16)
        padded = extended(normed, (("seq", 0),), 2)
        total = lax.cond(valid, convolve, skipped, padded)
        lifted = wide + jax.nn.gelu(total + bias, approximate=True)
        sent = lifted.astype(jnp.bfloat16)
        stored = lax.dynamic_update_index_in_dim(results, lifted, picked, 0)
        results = jnp.where(valid, stored, results)
        following = from_behind(sent, "segment", 1)
        return (following, results, joined)

    start = (
        jnp.zeros((rows, width), jnp.bfloat16),
        jnp.zeros((micro_count, rows, width), jnp.float32),
        jnp.zeros((micro_count, rows, width), jnp.bfloat16),
    )
    incoming, results, joined = lax.fori_loop(0, turns, turn, start)
    rounded = results.astype(jnp.bfloat16)
    joined = from_behind(rounded, "segment", segments - 1)
    final = (results + joined.astype(jnp.float32)).astype(jnp.bfloat16)
    output = jnp.where(segment == segments - 1, final, rounded)
    return output[None, None]


def per_device(activations, conv_weight, norm_gain, conv_bias):
    _, _, rows, width = activations.shape
    depth = conv_weight.shape[2]
    two_blocks = lax.axis_size("segment") == 2 and lax.axis_size("dp") == 4
    tiled = depth % EDGE == 0 and rows % EDGE == 0 and width % WIDE == 0
    fits = two_blocks and tiled and conv_weight.shape[1] // 2 <= EDGE and width > WIDE
    body = in_kernel if fits and lax.axis_size("seq") > 1 else relayed
    return body(activations, conv_weight, norm_gain, conv_bias)


def solution(mesh):
    in_specs = (
        P("dp", None, "seq", None),
        P("segment", None, ("dp", "seq"), None),
        P("segment", None),
        P("segment", None),
    )
    out_specs = P("segment", "dp", None, "seq", None)
    return jax.shard_map(
        per_device, mesh=mesh, in_specs=in_specs, out_specs=out_specs, check_vma=False
    )
```

```python
import functools

import jax
import jax.numpy as jnp
from jax import lax
from jax.experimental import pallas as pl
from jax.experimental.pallas import tpu as pltpu
from jax.sharding import PartitionSpec as P

EDGE = 16
HALF = 128
WIDE = 256


def kernel(
    seqs, act, weight, gain_in, bias_in, out,
    gain, bias, xin, halo, wbuf, padded, shifted,
    load_sem, gain_sem, bias_sem, own_sem, wsend, wrecv, hsend, hrecv, rsend, rrecv, esend, erecv,
):
    micros, rows, width = xin.shape
    taps = weight.shape[1]
    count = width // HALF
    dp = lax.axis_index("dp")
    seg = lax.axis_index("segment")
    z = lax.axis_index("seq")
    chip, core = dp // 2, dp % 2
    sib = chip * 2 + (1 - core)
    across = (1 - chip) * 2 + core
    has_up = z + 1 < seqs
    has_down = z > 0
    first = seg == 0

    ring = [lax.rem(z + d, seqs) for d in range(seqs)]
    ways = seqs + 1

    barrier = pltpu.get_barrier_semaphore()

    def greet(device):
        pl.semaphore_signal(barrier, inc=1, device_id=device, device_id_type=pl.DeviceIdType.MESH)

    greet((sib, seg, z))
    greet((across, seg, z))
    greet((dp, 1 - seg, z))
    for at in ring[1:]:
        greet((dp, seg, at))

    @pl.when(has_up)
    def _():
        greet((dp, 1 - seg, z + 1))

    @pl.when(has_down)
    def _():
        greet((dp, 1 - seg, z - 1))

    def piece(j, owner, at):
        return wbuf.at[j, owner * seqs + at]

    own_w = []
    for j in range(count):
        own_w.append(
            pltpu.make_async_copy(
                weight.at[0, :, :, pl.ds(j * HALF, HALF)], piece(j, dp, z), own_sem.at[j]
            )
        )
        own_w[-1].start()
    load_x = pltpu.make_async_copy(act.at[0], xin, load_sem)
    load_gain = pltpu.make_async_copy(gain_in, gain, gain_sem)
    load_bias = pltpu.make_async_copy(bias_in, bias, bias_sem)
    load_gain.start()
    load_bias.start()

    @pl.when(first)
    def _():
        load_x.start()

    ends = jnp.int32(has_up) + jnp.int32(has_down)
    pl.semaphore_wait(barrier, 2 + seqs + ends)

    pending = []

    def transfer(j, owner, at, slot, way):
        block = piece(j, owner, at)
        if way == 0:
            device = (sib, seg, z)
        elif way == 1:
            device = (across, seg, z)
        else:
            device = (dp, seg, ring[way - 1])
        return pltpu.make_async_remote_copy(
            src_ref=block,
            dst_ref=block,
            send_sem=wsend.at[j, slot * ways + way],
            recv_sem=wrecv.at[j, owner * seqs + at],
            device_id=device,
            device_id_type=pl.DeviceIdType.MESH,
        )

    def send(*piece_and_way):
        transfer(*piece_and_way).start()
        pending.append(piece_and_way)

    def arrive(j, owner, at):
        transfer(j, owner, at, 0, 0).wait_recv()

    def send_own(j):
        for way in [1, *range(2, ways), 0]:
            send(j, dp, z, 0, way)

    def from_column(j):
        for d in range(1, seqs):
            arrive(j, dp, ring[d])
            send(j, dp, ring[d], d, 1)
            send(j, dp, ring[d], d, 0)

    def from_across(j):
        for d in range(seqs):
            arrive(j, across, ring[d])
            send(j, across, ring[d], seqs + d, 0)

    def from_sibling(j):
        for at in ring:
            arrive(j, sib, at)
        for at in ring:
            arrive(j, (1 - chip) * 2 + (1 - core), at)

    def edge_in(side):
        up = side == 0
        return pltpu.make_async_remote_copy(
            src_ref=act.at[0, :, pl.ds(rows - EDGE if up else 0, EDGE), :],
            dst_ref=halo.at[side],
            send_sem=hsend.at[side],
            recv_sem=hrecv.at[side],
            device_id=(dp, seg, z + 1 if up else z - 1),
            device_id_type=pl.DeviceIdType.MESH,
        )

    def edge_out(j, side):
        up = side == 0
        cols = pl.ds(j * HALF, HALF)
        return pltpu.make_async_remote_copy(
            src_ref=out.at[0, 0, :, pl.ds(rows - EDGE if up else 0, EDGE), cols],
            dst_ref=halo.at[side, :, :, cols],
            send_sem=esend.at[j, side],
            recv_sem=erecv.at[j, side],
            device_id=(dp, 1 - seg, z + 1 if up else z - 1),
            device_id_type=pl.DeviceIdType.MESH,
        )

    def rows_out(j):
        cols = pl.ds(j * HALF, HALF)
        return pltpu.make_async_remote_copy(
            src_ref=out.at[0, 0, :, :, cols],
            dst_ref=xin.at[:, :, cols],
            send_sem=rsend.at[j],
            recv_sem=rrecv.at[j],
            device_id=(dp, 1 - seg, z),
            device_id_type=pl.DeviceIdType.MESH,
        )

    for side, cond in ((0, z == 0), (1, z == seqs - 1)):

        @pl.when(cond)
        def _():
            halo[side] = jnp.zeros(halo.shape[1:], halo.dtype)

    def normed(cells):
        wide = cells.astype(jnp.float32)
        stat = jnp.mean(wide * wide, axis=-1, keepdims=True)
        return wide * lax.rsqrt(stat + 1e-06) * gain[...]

    def shift_rows():
        def one(m, carry):
            padded[m, pl.ds(0, EDGE)] = normed(halo[0, m])
            padded[m, pl.ds(EDGE, rows)] = normed(xin[m])
            padded[m, pl.ds(EDGE + rows, EDGE)] = normed(halo[1, m])
            at = pl.multiple_of(m * rows, rows)
            for tap in range(taps):
                shifted[pl.ds(at, rows), pl.ds(tap * width, width)] = padded[
                    m, pl.ds(EDGE - taps // 2 + tap, rows), :
                ].astype(jnp.bfloat16)
            return carry

        lax.fori_loop(0, micros, one, 0)

    def convolve(*parts):
        kern = jnp.concatenate(
            [
                jnp.concatenate([wbuf[j, :, tap].reshape(width, HALF) for j in parts], axis=1)
                for tap in range(taps)
            ],
            axis=0,
        )
        return jnp.dot(shifted[...], kern, preferred_element_type=jnp.float32)

    def finish(total, c0, cw, join):
        cols = pl.ds(c0, cw)
        wide = xin[:, :, cols].astype(jnp.float32)
        total = total.reshape(micros, rows, cw) + bias[:, cols].reshape(1, 1, cw)
        lifted = wide + jax.nn.gelu(total, approximate=True)
        if join:
            lifted = lifted + wide
        out[0, 0, :, :, cols] = lifted.astype(out.dtype)

    def complete(j):
        from_across(j)
        from_sibling(j)

        @pl.when(first)
        def _():
            finish(convolve(j), j * HALF, HALF, False)
            rows_out(j).start()
            for side, cond in ((0, has_up), (1, has_down)):

                @pl.when(cond)
                def _():
                    edge_out(j, side).start()

    @pl.when(first)
    def _():
        for side, cond in ((0, has_up), (1, has_down)):

            @pl.when(cond)
            def _():
                edge_in(side).start()

    for j in range(2):
        own_w[j].wait()
        send_own(j)
    load_gain.wait()
    load_bias.wait()

    @pl.when(first)
    def _():
        load_x.wait()
        for side, cond in ((0, has_down), (1, has_up)):

            @pl.when(cond)
            def _():
                edge_in(side).wait_recv()

        shift_rows()

    for j in range(count):
        from_column(j)
        if j + 2 < count:
            own_w[j + 2].wait()
            send_own(j + 2)
        if j > 0:
            complete(j - 1)
    complete(count - 1)

    for piece_and_way in pending:
        transfer(*piece_and_way).wait_send()

    @pl.when(first)
    def _():
        for side, cond in ((0, has_up), (1, has_down)):

            @pl.when(cond)
            def _():
                edge_in(side).wait_send()
                for j in range(count):
                    edge_out(j, side).wait_send()

        for j in range(count):
            rows_out(j).wait_send()

    @pl.when(jnp.logical_not(first))
    def _():
        for j in range(count):
            rows_out(j).wait_recv()
        for side, cond in ((0, has_down), (1, has_up)):

            @pl.when(cond)
            def _():
                for j in range(count):
                    edge_out(j, side).wait_recv()

        shift_rows()
        for j in range(0, count, 2):
            finish(convolve(j, j + 1), j * HALF, WIDE, True)


def in_kernel(activations, conv_weight, norm_gain, conv_bias):
    _, micros, rows, width = activations.shape
    taps, depth = conv_weight.shape[1:3]
    seqs = lax.axis_size("seq")
    shards = lax.axis_size("dp") * seqs
    count = width // HALF
    dma = pltpu.SemaphoreType.DMA
    vmem = pl.BlockSpec(memory_space=pltpu.VMEM)
    anywhere = pl.BlockSpec(memory_space=pl.ANY)
    flops = 2 * micros * rows * taps * width * width
    return pl.pallas_call(
        functools.partial(kernel, seqs),
        out_shape=jax.ShapeDtypeStruct((1, 1, micros, rows, width), jnp.bfloat16),
        in_specs=[anywhere] * 4,
        out_specs=vmem,
        scratch_shapes=[
            pltpu.VMEM((1, width), jnp.float32),
            pltpu.VMEM((1, width), jnp.float32),
            pltpu.VMEM((micros, rows, width), jnp.bfloat16),
            pltpu.VMEM((2, micros, EDGE, width), jnp.bfloat16),
            pltpu.VMEM((count, shards, taps, depth, HALF), jnp.bfloat16),
            pltpu.VMEM((micros, rows + 2 * EDGE, width), jnp.float32),
            pltpu.VMEM((micros * rows, taps * width), jnp.bfloat16),
            dma,
            dma,
            dma,
            dma((count,)),
            dma((count, 2 * seqs * (seqs + 1))),
            dma((count, shards)),
            dma((2,)),
            dma((2,)),
            dma((count,)),
            dma((count,)),
            dma((count, 2)),
            dma((count, 2)),
        ],
        cost_estimate=pl.CostEstimate(
            flops=flops, bytes_accessed=4 * activations.size, transcendentals=micros * rows * width
        ),
        compiler_params=pltpu.CompilerParams(
            collective_id=0, has_side_effects=True, vmem_limit_bytes=60 * 1024 * 1024
        ),
    )(activations, conv_weight, norm_gain, conv_bias)


def extended(cells, sides, width):
    for axis, dim in sides:
        count = lax.axis_size(axis)
        ends = count - 1
        head = lax.slice_in_dim(cells, 0, width, axis=dim)
        tail = lax.slice_in_dim(cells, cells.shape[dim] - width, cells.shape[dim], axis=dim)
        cells = jnp.concatenate(
            [
                lax.ppermute(tail, axis, [(i, (i + 1) % count) for i in range(ends)]),
                cells,
                lax.ppermute(head, axis, [((i + 1) % count, i) for i in range(ends)]),
            ],
            axis=dim,
        )
    return cells


def from_behind(block, axis, distance):
    devices = range(lax.axis_size(axis))
    route = [(i - distance, i) for i in devices if i - distance in devices]
    return lax.ppermute(block, axis, route)


def relayed(activations, conv_weight, norm_gain, conv_bias):
    kernel = lax.all_gather(conv_weight, ("dp", "seq"), axis=2, tiled=True)[0]
    gain = norm_gain[0]
    bias = conv_bias[0]
    inputs = activations[0]
    micro_count = inputs.shape[0]
    rows = inputs.shape[1]
    width = inputs.shape[2]
    segments = lax.axis_size("segment")
    segment = lax.axis_index("segment")
    turns = segments + micro_count - 1
    taps = kernel.shape[0]

    def convolve(padded):
        total = jnp.zeros((rows, width), jnp.float32)
        for tap in range(taps):
            total = total + jnp.dot(
                padded[tap : tap + rows], kernel[tap], preferred_element_type=jnp.float32
            )
        return total

    def skipped(padded):
        return jnp.zeros((rows, width), jnp.float32)

    def turn(step, carry):
        incoming, results, joined = carry
        micro = step - segment
        valid = jnp.logical_and(micro >= 0, micro < micro_count)
        picked = jnp.clip(micro, 0, micro_count - 1)
        own = lax.dynamic_index_in_dim(inputs, picked, 0, keepdims=False)
        current = jnp.where(segment == 0, own, incoming)
        wide = current.astype(jnp.float32)
        stat = jnp.mean(wide * wide, axis=-1, keepdims=True)
        normed = (wide / jnp.sqrt(stat + 1e-06) * gain).astype(jnp.bfloat16)
        padded = extended(normed, (("seq", 0),), 2)
        total = lax.cond(valid, convolve, skipped, padded)
        lifted = wide + jax.nn.gelu(total + bias, approximate=True)
        sent = lifted.astype(jnp.bfloat16)
        stored = lax.dynamic_update_index_in_dim(results, lifted, picked, 0)
        results = jnp.where(valid, stored, results)
        following = from_behind(sent, "segment", 1)
        return (following, results, joined)

    start = (
        jnp.zeros((rows, width), jnp.bfloat16),
        jnp.zeros((micro_count, rows, width), jnp.float32),
        jnp.zeros((micro_count, rows, width), jnp.bfloat16),
    )
    incoming, results, joined = lax.fori_loop(0, turns, turn, start)
    rounded = results.astype(jnp.bfloat16)
    joined = from_behind(rounded, "segment", segments - 1)
    final = (results + joined.astype(jnp.float32)).astype(jnp.bfloat16)
    output = jnp.where(segment == segments - 1, final, rounded)
    return output[None, None]


def per_device(activations, conv_weight, norm_gain, conv_bias):
    _, _, rows, width = activations.shape
    depth = conv_weight.shape[2]
    two_blocks = lax.axis_size("segment") == 2 and lax.axis_size("dp") == 4
    tiled = depth % EDGE == 0 and rows % EDGE == 0 and width % WIDE == 0
    fits = two_blocks and tiled and conv_weight.shape[1] // 2 <= EDGE and width > WIDE
    body = in_kernel if fits and lax.axis_size("seq") > 1 else relayed
    return body(activations, conv_weight, norm_gain, conv_bias)


def solution(mesh):
    in_specs = (
        P("dp", None, "seq", None),
        P("segment", None, ("dp", "seq"), None),
        P("segment", None),
        P("segment", None),
    )
    out_specs = P("segment", "dp", None, "seq", None)
    return jax.shard_map(
        per_device, mesh=mesh, in_specs=in_specs, out_specs=out_specs, check_vma=False
    )
```
